128 devices in a mesh: dp: 16 (over x, z), tensor: 8 (over y, core).
Axes of the slice: x: 4, y: 4, z: 4, core: 2. Of those that a mesh axis runs over, the one named last changes fastest.
Arguments:
- gradients: bfloat16 [16, 2304, 24576], P('dp', None, 'tensor'), as said below
- dither: int32 [16, 2304], P('dp'), may hold values from 0 to 1023
- sign_bits: int32 [24576], P('tensor'), may hold values from 0 to 1
Outputs:
- mean_gradient: bfloat16 [2304, 24576], P('dp', 'tensor')
The draws below stay inside these ranges and needn't reach their ends.
Inputs may be any that keep to these rules, and one draw needn't show every extreme that they name: `gradients`: one gradient matrix a replica; entries bounded.
All inputs are finite; a program needn't handle non-finite values.
Results may differ from the reference program's by a relative error of at most 0.006.
Values may be sent and summed in bfloat16 or wider, within the bound.
A program may use at most 192 MiB of HBM per device.

```python
import jax
import jax.numpy as jnp
from jax import lax

ROWS = 2304
COLS = 24576
BLOCK = 1024
LEVELS = 127
REPLICAS = 16


def draw_gradients(key, part):
    key = jax.random.fold_in(key, 5)
    key_base = jax.random.fold_in(key, 0)
    key_rows = jax.random.fold_in(key, 1)
    key_order_r = jax.random.fold_in(key, 3)
    key_order_c = jax.random.fold_in(key, 4)
    block_count = COLS // BLOCK
    replica_order = jax.random.permutation(key_order_r, REPLICAS)
    block_order = jax.random.permutation(key_order_c, block_count)
    replica_pos = replica_order.astype(jnp.float32) / max(REPLICAS - 1, 1)
    block_pos = block_order.astype(jnp.float32) / max(block_count - 1, 1)
    column_pos = jnp.repeat(block_pos, BLOCK)
    row_scale = 10.0 ** (jax.random.uniform(key_rows, (1, ROWS, 1), dtype=jnp.float32) - 0.5)
    values = jnp.clip(jax.random.normal(key_base, (REPLICAS, ROWS, COLS), dtype=jnp.float32), -4.0, 4.0)
    ramp = 3.0 ** (replica_pos[:, None, None] + column_pos[None, None, :])
    return (0.5 * values * ramp * row_scale).astype(jnp.bfloat16)


def touch_ends(result, key, smallest, largest):
    spot = [jax.random.randint(jax.random.fold_in(key, axis), (), 0, length) for axis, length in enumerate(result.shape)]
    main_axis = result.shape.index(max(result.shape))
    next_to = spot[:main_axis] + [(spot[main_axis] + 1) % result.shape[main_axis]] + spot[main_axis + 1:]
    return result.at[tuple(spot)].set(smallest).at[tuple(next_to)].set(largest)


def setup_inputs(seed: int = 0) -> dict:
    streams_of = jax.random.split(jax.random.key(seed), 4)
    gradients = draw_gradients(jax.random.fold_in(streams_of[3], 71), 0)
    dither = touch_ends(jax.random.randint(streams_of[1], (REPLICAS, ROWS), 0, BLOCK), jax.random.fold_in(streams_of[1], 1), 0, BLOCK - 1).astype(jnp.int32)
    sign_bits = touch_ends(jax.random.randint(streams_of[2], (COLS,), 0, 2), jax.random.fold_in(streams_of[2], 1), 0, 1).astype(jnp.int32)
    return {"gradients": gradients, "dither": dither, "sign_bits": sign_bits}


def hadamard(values):
    length = values.shape[-1]
    stride = 1
    while stride < length:
        shaped = values.reshape(values.shape[:-1] + (length // (2 * stride), 2, stride))
        front_half = shaped[..., 0, :]
        back_half = shaped[..., 1, :]
        values = jnp.stack([front_half + back_half, front_half - back_half], axis=-2).reshape(values.shape)
        stride = stride * 2
    return values


def reference(gradients, dither, sign_bits):
    flips = 1.0 - 2.0 * sign_bits.astype(jnp.float32)

    def rotate(gradient):
        return hadamard((gradient.astype(jnp.float32) * flips).reshape(ROWS, COLS // BLOCK, BLOCK))

    peaks = lax.map(lambda gradient: jnp.max(jnp.abs(rotate(gradient))), gradients)
    global_peak = jnp.max(peaks)
    position = jnp.arange(BLOCK, dtype=jnp.int32)

    def accumulate(summed, inputs):
        gradient, offsets = inputs
        uniform = (((offsets[:, None, None] + 7919 * position[None, None, :]) % BLOCK).astype(jnp.float32) + 0.5) / BLOCK
        quantized = jnp.floor(rotate(gradient) * (LEVELS / global_peak) + uniform)
        return summed + quantized, None

    start = jnp.zeros((ROWS, COLS // BLOCK, BLOCK), jnp.float32)
    summed, _ = lax.scan(accumulate, start, (gradients, dither))
    decoded = hadamard(summed) * (global_peak / (LEVELS * REPLICAS * BLOCK))
    return (decoded.reshape(ROWS, COLS) * flips).astype(jnp.bfloat16)
```

```python
import functools

import jax
import jax.numpy as jnp
from jax import lax
from jax.experimental import pallas as pl
from jax.experimental.pallas import tpu as pltpu
from jax.sharding import PartitionSpec as P

BLOCK = 1024
LEVELS = 127
SIDE = 4
SUB = 256
LANES = 128
MESH = pl.DeviceIdType.MESH

GROUPS = ((0, 0, 0, 144, 0), (1, 2, 0, 144, 224), (0, 1, 0, 80, 144), (1, 1, 80, 64, 368))
PIECES = (
    (0, 0, 0, 48, 0), (1, 2, 0, 48, 224),
    (0, 0, 48, 48, 48), (1, 2, 48, 48, 272),
    (0, 0, 96, 48, 96), (1, 2, 96, 48, 320),
    (0, 1, 0, 48, 144), (1, 1, 80, 32, 368),
    (0, 1, 48, 32, 192), (1, 1, 112, 32, 400),
)
ROWS = 432


def butterfly(parts):
    a, b = parts[0] + parts[1], parts[0] - parts[1]
    c, d = parts[2] + parts[3], parts[2] - parts[3]
    return [a + c, b + d, a - c, b - d]


def kernel(grad, dither_ref, sign_ref, out_ref, held, weights, table, own_dither, near_raw, near_dither, ramp, peak_send,
           peak_recv, peak_ref, raw, first_send, first_recv, partial, second_raw, second_send, second_recv,
           load_sem, near_ss, near_rs, peak_ss, peak_rs, raw_ss, raw_rs, first_ss, first_rs, mid_ss, mid_rs, last_ss, last_rs):
    dp, tensor = lax.axis_index("dp"), lax.axis_index("tensor")
    x, z = dp // SIDE, dp % SIDE

    def along_x(step):
        return ((x + step) % SIDE * SIDE + z, tensor)

    def along_z(step):
        return (x * SIDE + (z + step) % SIDE, tensor)

    def neighbour(axis, step):
        return along_x(step) if axis == 0 else along_z(step)

    stages = (
        [(dp, (tensor + i) % 8) for i in range(1, 8)],
        [along_x(i) for i in range(1, SIDE)],
        [along_z(i) for i in range(1, SIDE)],
    )
    barrier = pltpu.get_barrier_semaphore()
    for stage in stages:
        for peer in stage:
            pl.semaphore_signal(barrier, inc=1, device_id=peer, device_id_type=MESH)

    def load(c):
        return pltpu.make_async_copy(grad.at[c // SIDE, c % SIDE], held.at[c // SIDE, c % SIDE], load_sem.at[c])

    def start_load(c, carry):
        load(c).start()
        return carry

    lax.fori_loop(0, SIDE * SIDE, start_load, 0)

    bits = lax.broadcasted_iota(jnp.int32, (SUB, SUB), 0) & lax.broadcasted_iota(jnp.int32, (SUB, SUB), 1)
    bits = bits ^ (bits >> 4)
    bits = bits ^ (bits >> 2)
    bits = bits ^ (bits >> 1)
    base = (1 - 2 * (bits & 1)).astype(jnp.float32).astype(jnp.bfloat16)
    table[...] = base
    diagonal = lax.broadcasted_iota(jnp.int32, (SUB, SUB), 0) == lax.broadcasted_iota(jnp.int32, (SUB, SUB), 1)
    for i in range(12):
        flips = (1 - 2 * sign_ref[:, i * SUB:(i + 1) * SUB]).astype(jnp.float32)
        scaled = jnp.where(diagonal, flips, 0.0).astype(jnp.bfloat16)
        weights[i // SIDE, i % SIDE] = jnp.dot(scaled, base, preferred_element_type=jnp.float32).astype(jnp.bfloat16)
    column = lax.broadcasted_iota(jnp.int32, (1, BLOCK), 1)
    ramp[...] = (((7919 * column) & (BLOCK - 1)).astype(jnp.float32) + 0.5) * (1.0 / BLOCK)

    pl.semaphore_wait(barrier, 13)

    raw_copies = []
    for g, (h, b, r0, n, q) in enumerate(GROUPS):
        far = (x + 2) % SIDE if h == 0 else (z + 2) % SIDE
        for e in range(2):
            pair = pl.ds(2 * e, 2)
            rows, cols = pl.ds(r0, n), pl.ds(b * BLOCK, BLOCK)
            source = grad.at[far, pair, rows, cols] if h == 0 else grad.at[pair, far, rows, cols]
            copy = pltpu.make_async_remote_copy(
                source, raw.at[e, :, pl.ds(q, n), :], raw_ss.at[2 * g + e], raw_rs.at[2 * g + e],
                device_id=neighbour(h, 2 * e - 1), device_id_type=MESH)
            copy.start()
            raw_copies.append(copy)
    near_copies = []
    for i in range(4):
        copy = pltpu.make_async_remote_copy(
            dither_ref, near_raw.at[i], near_ss.at[i], near_rs.at[i],
            device_id=neighbour(i // 2, 2 * (i % 2) - 1), device_id_type=MESH)
        copy.start()
        near_copies.append(copy)

    def parts_of(ref, lead, rows, b, first):
        return [
            jnp.dot(ref[lead + (rows, pl.ds(first + k * SUB, SUB))], weights[b, k], preferred_element_type=jnp.float32)
            for k in range(SIDE)
        ]

    def peak_of(c, top):
        load(c).wait()
        for b in range(3):
            m = parts_of(held, (c // SIDE, c % SIDE), slice(None), b, b * BLOCK)
            even = jnp.abs(m[0] + m[1]) + jnp.abs(m[2] + m[3])
            odd = jnp.abs(m[0] - m[1]) + jnp.abs(m[2] - m[3])
            both = jnp.maximum(even, odd)
            both = jnp.maximum(both[:, :LANES], both[:, LANES:])
            top = jnp.maximum(top, jnp.max(both.reshape(18, 8, LANES), axis=0))
        return top

    top = lax.fori_loop(0, SIDE * SIDE, peak_of, jnp.zeros((8, LANES), jnp.float32))

    def spread(source, target):
        turned = jnp.transpose(source, (1, 0))[:144]
        for c in range(SIDE * SIDE):
            target[c // SIDE, c % SIDE] = jnp.broadcast_to(turned[:, c:c + 1], (144, LANES))

    done = 0
    peak_copies = []
    for s, stage in enumerate(stages):
        peak_send[s] = top
        copies = []
        for i, peer in enumerate(stage):
            copy = pltpu.make_async_remote_copy(
                peak_send.at[s], peak_recv.at[done + i], peak_ss.at[done + i], peak_rs.at[done + i],
                device_id=peer, device_id_type=MESH)
            copy.start()
            copies.append(copy)
        if s == 0:
            spread(dither_ref[...], own_dither)
            for i in range(4):
                near_copies[i].wait_recv()
                spread(near_raw[i], near_dither.at[i])
        for i, copy in enumerate(copies):
            copy.wait_recv()
        for i in range(len(stage)):
            top = jnp.maximum(top, peak_recv[done + i])
        done += len(stage)
        peak_copies += copies
    top = jnp.max(jnp.max(top, axis=1, keepdims=True), axis=0, keepdims=True)
    peak = jnp.broadcast_to(top, (8, LANES))
    peak_ref[0] = LEVELS / peak
    peak_ref[1] = peak / (LEVELS * 16 * BLOCK)

    def codes(ref, lead, rows, b, first, offsets):
        values = butterfly(parts_of(ref, lead, rows, b, first))
        scale = peak_ref[0, 0:1, :]
        result = []
        for i in range(8):
            shift = offsets + ramp[:, i * LANES:(i + 1) * LANES]
            shift = shift - jnp.floor(shift)
            value = values[i // 2][:, (i % 2) * LANES:(i % 2 + 1) * LANES]
            result.append(jnp.floor(value * scale + shift))
        return result

    def own_codes(h, target, j, b, r0, n):
        lead = (target, j) if h == 0 else (j, target)
        rows = pl.ds(r0, n)
        return codes(held, lead, rows, b, b * BLOCK, own_dither[lead + (rows, slice(None))])

    def lanes(i):
        return slice(i * LANES, (i + 1) * LANES)

    for copy in raw_copies:
        copy.wait_recv()

    first_copies = []
    for p, (h, b, r0, n, q) in enumerate(PIECES):
        here = x if h == 0 else z
        for e in range(2):
            target = (here + 2 * e + 3) % SIDE

            def fill(jj, carry):
                j = 2 * e + jj
                mine = own_codes(h, target, j, b, r0, n)
                lead = (target, j) if h == 0 else (j, target)
                other = codes(raw, (e, jj), pl.ds(q, n), b, 0, near_dither[(2 * h + e,) + lead + (pl.ds(r0, n), slice(None))])
                for i in range(8):
                    first_send[e, j, pl.ds(q, n), lanes(i)] = (mine[i] + other[i]).astype(jnp.bfloat16)
                j = 2 * (1 - e) + jj
                mine = own_codes(h, target, j, b, r0, n)
                for i in range(8):
                    first_send[e, j, pl.ds(q, n), lanes(i)] = mine[i].astype(jnp.bfloat16)
                return carry

            lax.fori_loop(0, 2, fill, 0)
            copy = pltpu.make_async_remote_copy(
                first_send.at[e, :, pl.ds(q, n), :], first_recv.at[e, :, pl.ds(q, n), :],
                first_ss.at[2 * p + e], first_rs.at[2 * p + e],
                device_id=neighbour(h, 2 * e - 1), device_id_type=MESH)
            copy.start()
            first_copies.append(copy)

    mid_copies, last_copies = [], []

    def combine(p):
        h, b, r0, n, q = PIECES[p]
        here, there = (x, z) if h == 0 else (z, x)
        rows = pl.ds(q, n)
        for e in range(2):
            first_copies[2 * p + e].wait_recv()

        def fill(jj, carry):
            j = (there + 2 + jj) % SIDE
            mine = own_codes(h, here, j, b, r0, n)
            for i in range(8):
                total = mine[i]
                for e in range(2):
                    total += first_recv[e, j, rows, lanes(i)].astype(jnp.float32)
                partial[j, rows, lanes(i)] = total.astype(jnp.int32).astype(jnp.int16)
            return carry

        lax.fori_loop(0, 1, fill, 0)
        for e in range(2):
            copy = pltpu.make_async_remote_copy(
                partial.at[(there + 2) % SIDE, rows, pl.ds(512 * e, 512)], second_raw.at[e, rows, :],
                mid_ss.at[2 * p + e], mid_rs.at[2 * p + e],
                device_id=neighbour(1 - h, 2 * e - 1), device_id_type=MESH)
            copy.start()
            mid_copies.append(copy)
        lax.fori_loop(1, SIDE, fill, 0)

    def forward(p):
        h, b, r0, n, q = PIECES[p]
        there = z if h == 0 else x
        rows = pl.ds(q, n)
        for e in range(2):
            mid_copies[2 * p + e].wait_recv()
            j = (there + 2 * e + 3) % SIDE
            plain, summed = pl.ds(512 * (1 - e), 512), pl.ds(512 * e, 512)
            second_send[e, rows, plain] = partial[j, rows, plain]
            total = partial[j, rows, summed].astype(jnp.int32) + second_raw[e, rows, :].astype(jnp.int32)
            second_send[e, rows, summed] = total.astype(jnp.int16)
            copy = pltpu.make_async_remote_copy(
                second_send.at[e, rows, :], second_recv.at[e, rows, :],
                last_ss.at[2 * p + e], last_rs.at[2 * p + e],
                device_id=neighbour(1 - h, 2 * e - 1), device_id_type=MESH)
            copy.start()
            last_copies.append(copy)

    def decode(p):
        h, b, r0, n, q = PIECES[p]
        there = z if h == 0 else x
        rows = pl.ds(q, n)
        for e in range(2):
            last_copies[2 * p + e].wait_recv()
        parts = []
        for k in range(SIDE):
            cols = pl.ds(k * SUB, SUB)
            total = partial[there, rows, cols].astype(jnp.int32)
            for e in range(2):
                total += second_recv[e, rows, cols].astype(jnp.int32)
            total = total.astype(jnp.float32)
            high = total.astype(jnp.bfloat16)
            low = (total - high.astype(jnp.float32)).astype(jnp.bfloat16)
            parts.append(jnp.dot(high, table[...], preferred_element_type=jnp.float32)
                         + jnp.dot(low, table[...], preferred_element_type=jnp.float32))
        values = butterfly(parts)
        factor = peak_ref[1, 0:1, :]
        for i in range(8):
            col = b * BLOCK + i * LANES
            flips = (1 - 2 * sign_ref[:, col:col + LANES]).astype(jnp.float32)
            value = values[i // 2][:, (i % 2) * LANES:(i % 2 + 1) * LANES]
            out_ref[r0:r0 + n, col:col + LANES] = (value * factor * flips).astype(jnp.bfloat16)

    count = len(PIECES)
    for step in range(count + 4):
        if step < count:
            combine(step)
        if 2 <= step < count + 2:
            forward(step - 2)
        if step >= 4:
            decode(step - 4)
    for copy in near_copies + peak_copies + raw_copies + first_copies + mid_copies + last_copies:
        copy.wait_send()


def local(gradients, dither, sign_bits):
    row_count, col_count = gradients.shape[1:]
    grad = gradients.reshape(SIDE, SIDE, row_count // 16, col_count)
    offsets = jnp.pad(dither.astype(jnp.float32).reshape(16, row_count // 16) * (1.0 / BLOCK), ((0, 0), (0, 112)))
    vmem, dma = pltpu.VMEM, pltpu.SemaphoreType.DMA
    pieces = 2 * len(PIECES)
    return pl.pallas_call(
        kernel,
        out_shape=jax.ShapeDtypeStruct((row_count // 16, col_count), jnp.bfloat16),
        in_specs=[pl.BlockSpec(memory_space=pl.ANY)] + [pl.BlockSpec(memory_space=pltpu.VMEM)] * 2,
        out_specs=pl.BlockSpec(memory_space=pltpu.VMEM),
        scratch_shapes=[
            vmem((SIDE, SIDE, 144, col_count), jnp.bfloat16),
            vmem((3, SIDE, SUB, SUB), jnp.bfloat16),
            vmem((SUB, SUB), jnp.bfloat16),
            vmem((SIDE, SIDE, 144, LANES), jnp.float32),
            vmem((4, 16, 256), jnp.float32),
            vmem((4, SIDE, SIDE, 144, LANES), jnp.float32),
            vmem((1, BLOCK), jnp.float32),
            vmem((3, 8, LANES), jnp.float32),
            vmem((13, 8, LANES), jnp.float32),
            vmem((2, 8, LANES), jnp.float32),
            vmem((2, 2, ROWS, BLOCK), jnp.bfloat16),
            vmem((2, SIDE, ROWS, BLOCK), jnp.bfloat16),
            vmem((2, SIDE, ROWS, BLOCK), jnp.bfloat16),
            vmem((SIDE, ROWS, BLOCK), jnp.int16),
            vmem((2, ROWS, 512), jnp.int16),
            vmem((2, ROWS, BLOCK), jnp.int16),
            vmem((2, ROWS, BLOCK), jnp.int16),
            dma((16,)), dma((4,)), dma((4,)), dma((13,)), dma((13,)), dma((8,)), dma((8,)),
            dma((pieces,)), dma((pieces,)), dma((pieces,)), dma((pieces,)), dma((pieces,)), dma((pieces,)),
        ],
        compiler_params=pltpu.CompilerParams(collective_id=0, has_side_effects=True, vmem_limit_bytes=60 * 2**20),
    )(grad, offsets, sign_bits.reshape(1, col_count))


def solution(mesh):
    return jax.shard_map(
        local,
        mesh=mesh,
        in_specs=(P("dp", None, "tensor"), P("dp", None), P("tensor")),
        out_specs=P("dp", "tensor"),
        check_vma=False,
    )
```

```python
import functools

import jax
import jax.numpy as jnp
from jax import lax
from jax.experimental import pallas as pl
from jax.experimental.pallas import tpu as pltpu
from jax.sharding import PartitionSpec as P

BLOCK = 1024
LEVELS = 127
SIDE = 4
SUB = 256
LANES = 128
MESH = pl.DeviceIdType.MESH

PIECES = (
    (0, 0, 0, 48, 0), (1, 2, 0, 48, 224),
    (0, 0, 48, 48, 48), (1, 2, 48, 48, 272),
    (0, 0, 96, 48, 96), (1, 2, 96, 48, 320),
    (0, 1, 0, 48, 144), (1, 1, 80, 32, 368),
    (0, 1, 48, 32, 192), (1, 1, 112, 32, 400),
)
ROWS = 432
RAW_EARLY = (0, 1, 2, 3, 4, 5, 7)
RAW_LATER = ((), (6, 8), (9,))
LEAVES = {0: 0, 1: 48}
LEAF_LATER = ((), (0,), (1,))
LEAF_ROWS = 96


def butterfly(parts):
    a, b = parts[0] + parts[1], parts[0] - parts[1]
    c, d = parts[2] + parts[3], parts[2] - parts[3]
    return [a + c, b + d, a - c, b - d]


def kernel(grad, dither_in, sign_in, out_ref, dither_ref, sign_ref, held, weights, table, own_dither, near_raw, near_dither, rows_of, ramp, peak_send,
           peak_recv, peak_ref, raw, leaf, first_send, first_recv, partial, second_raw, second_send, second_recv,
           small_sem, load_sem, near_ss, near_rs, peak_ss, peak_rs, raw_ss, raw_rs, leaf_ss, leaf_rs, first_ss, first_rs, mid_ss, mid_rs, last_ss, last_rs):
    dp, tensor = lax.axis_index("dp"), lax.axis_index("tensor")
    x, z = dp // SIDE, dp % SIDE

    def lanes(i):
        return slice(i * LANES, (i + 1) * LANES)

    def along_x(step):
        return ((x + step) % SIDE * SIDE + z, tensor)

    def along_z(step):
        return (x * SIDE + (z + step) % SIDE, tensor)

    def neighbour(axis, step):
        return along_x(step) if axis == 0 else along_z(step)

    stages = (
        [(dp, (tensor + i) % 8) for i in range(1, 8)],
        [along_x(i) for i in range(1, SIDE)],
        [along_z(i) for i in range(1, SIDE)],
    )
    small = [pltpu.make_async_copy(dither_in, dither_ref, small_sem.at[0]),
             pltpu.make_async_copy(sign_in, sign_ref, small_sem.at[1])]
    for copy in small:
        copy.start()
    barrier = pltpu.get_barrier_semaphore()
    for stage in stages:
        for peer in stage:
            pl.semaphore_signal(barrier, inc=1, device_id=peer, device_id_type=MESH)

    def load(c):
        return pltpu.make_async_copy(grad.at[c // SIDE, c % SIDE], held.at[c // SIDE, c % SIDE], load_sem.at[c])

    def start_load(c, carry):
        load(c).start()
        return carry

    lax.fori_loop(0, SIDE * SIDE, start_load, 0)

    pl.semaphore_wait(barrier, 13)

    raw_copies = {}

    def send_raw(p):
        h, b, r0, n, q = PIECES[p]
        far = (x + 2) % SIDE if h == 0 else (z + 2) % SIDE
        for e in range(2):
            pair = pl.ds(2 * e, 2)
            rows, cols = pl.ds(r0, n), pl.ds(b * BLOCK, BLOCK)
            source = grad.at[far, pair, rows, cols] if h == 0 else grad.at[pair, far, rows, cols]
            copy = pltpu.make_async_remote_copy(
                source, raw.at[e, :, pl.ds(q, n), :], raw_ss.at[2 * p + e], raw_rs.at[2 * p + e],
                device_id=neighbour(h, 2 * e - 1), device_id_type=MESH)
            copy.start()
            raw_copies[2 * p + e] = copy

    leaf_copies = {}

    def send_leaf(p):
        h, b, r0, n, q = PIECES[p]
        here = x if h == 0 else z
        for e in range(2):
            target = (here + 2 * e + 3) % SIDE
            pair = pl.ds(2 * (1 - e), 2)
            rows, cols = pl.ds(r0, n), pl.ds(b * BLOCK, BLOCK)
            source = grad.at[target, pair, rows, cols] if h == 0 else grad.at[pair, target, rows, cols]
            copy = pltpu.make_async_remote_copy(
                source, leaf.at[e, :, pl.ds(LEAVES[p], n), :], leaf_ss.at[2 * p + e], leaf_rs.at[2 * p + e],
                device_id=neighbour(h, 2 * e - 1), device_id_type=MESH)
            copy.start()
            leaf_copies[2 * p + e] = copy

    small[0].wait()
    near_copies = []
    for i in range(4):
        copy = pltpu.make_async_remote_copy(
            dither_ref, near_raw.at[i], near_ss.at[i], near_rs.at[i],
            device_id=neighbour(i // 2, 2 * (i % 2) - 1), device_id_type=MESH)
        copy.start()
        near_copies.append(copy)

    for p in RAW_EARLY:
        send_raw(p)

    bits = lax.broadcasted_iota(jnp.int32, (SUB, SUB), 0) & lax.broadcasted_iota(jnp.int32, (SUB, SUB), 1)
    bits = bits ^ (bits >> 4)
    bits = bits ^ (bits >> 2)
    bits = bits ^ (bits >> 1)
    base = (1 - 2 * (bits & 1)).astype(jnp.float32).astype(jnp.bfloat16)
    table[...] = base
    small[1].wait()
    diagonal = lax.broadcasted_iota(jnp.int32, (SUB, SUB), 0) == lax.broadcasted_iota(jnp.int32, (SUB, SUB), 1)
    for i in range(12):
        flips = (1 - 2 * sign_ref[:, i * SUB:(i + 1) * SUB]).astype(jnp.float32)
        scaled = jnp.where(diagonal, flips, 0.0).astype(jnp.bfloat16)
        weights[i // SIDE, i % SIDE] = jnp.dot(scaled, base, preferred_element_type=jnp.float32).astype(jnp.bfloat16)
    column = lax.broadcasted_iota(jnp.int32, (1, BLOCK), 1)
    ramp[...] = (((7919 * column) & (BLOCK - 1)).astype(jnp.float32) + 0.5) * (1.0 / BLOCK)

    def parts_of(ref, lead, b, first):
        parts = []
        for k in range(SIDE):
            values = ref[lead + (pl.ds(first + k * SUB, SUB),)]
            values = values.reshape(-1, SUB)
            parts.append(jnp.dot(values, weights[b, k], preferred_element_type=jnp.float32))
        return parts

    def peak_of(c, top):
        load(2 * c).wait()
        load(2 * c + 1).wait()
        for b in range(3):
            m = parts_of(held, (c // 2, pl.ds(c % 2 * 2, 2), slice(None)), b, b * BLOCK)
            even = jnp.abs(m[0] + m[1]) + jnp.abs(m[2] + m[3])
            odd = jnp.abs(m[0] - m[1]) + jnp.abs(m[2] - m[3])
            both = jnp.maximum(even, odd)
            both = jnp.maximum(both[:, :LANES], both[:, LANES:])
            top = jnp.maximum(top, jnp.max(both.reshape(36, 8, LANES), axis=0))
        return top

    top = lax.fori_loop(0, SIDE * 2, peak_of, jnp.zeros((8, LANES), jnp.float32))

    def spread(source, target):
        for i in range(18):
            rows_of[i:i + 1, :] = source[:, lanes(i)].astype(jnp.float32) * (1.0 / BLOCK)
        turned = jnp.transpose(rows_of[...], (1, 0))
        for i in range(18):
            spread_rows = jnp.broadcast_to(turned[:, i:i + 1], (LANES, LANES))
            start = i * LANES
            while start < (i + 1) * LANES:
                c, r = start // 144, start % 144
                n = min(144 - r, (i + 1) * LANES - start)
                target[c // SIDE, c % SIDE, r:r + n, :] = spread_rows[start - i * LANES:start - i * LANES + n]
                start += n

    done = 0
    peak_copies = []
    for s, stage in enumerate(stages):
        peak_send[s] = top
        copies = []
        for i, peer in enumerate(stage):
            copy = pltpu.make_async_remote_copy(
                peak_send.at[s], peak_recv.at[done + i], peak_ss.at[done + i], peak_rs.at[done + i],
                device_id=peer, device_id_type=MESH)
            copy.start()
            copies.append(copy)
        for p in RAW_LATER[s]:
            send_raw(p)
        for p in LEAF_LATER[s]:
            send_leaf(p)
        if s == 0:
            spread(dither_ref, own_dither)
            for i in range(4):
                near_copies[i].wait_recv()
                spread(near_raw.at[i], near_dither.at[i])
        for i, copy in enumerate(copies):
            copy.wait_recv()
        for i in range(len(stage)):
            top = jnp.maximum(top, peak_recv[done + i])
        done += len(stage)
        peak_copies += copies
    top = jnp.max(jnp.max(top, axis=1, keepdims=True), axis=0, keepdims=True)
    peak = jnp.broadcast_to(top, (8, LANES))
    peak_ref[0] = LEVELS / peak
    peak_ref[1] = peak / (LEVELS * 16 * BLOCK)

    def codes(ref, lead, b, first, offsets):
        values = butterfly(parts_of(ref, lead, b, first))
        offsets = offsets.reshape(-1, LANES)
        scale = peak_ref[0, 0:1, :]
        result = []
        for i in range(8):
            shift = offsets + ramp[:, lanes(i)]
            shift = shift - jnp.floor(shift)
            value = values[i // 2][:, (i % 2) * LANES:(i % 2 + 1) * LANES]
            result.append(jnp.floor(value * scale + shift))
        return result

    def pair_of(h, target, j, r0, n):
        pair = pl.ds(j, 2)
        return ((target, pair) if h == 0 else (pair, target)) + (pl.ds(r0, n),)

    def own_codes(h, target, j, b, r0, n):
        lead = pair_of(h, target, j, r0, n)
        return codes(held, lead, b, b * BLOCK, own_dither[lead + (slice(None),)])

    def near_codes(ref, lead, h, e, target, j, b, r0, n):
        return codes(ref, lead, b, 0, near_dither[(2 * h + e,) + pair_of(h, target, j, r0, n) + (slice(None),)])

    first_copies = {}

    def first(p):
        h, b, r0, n, q = PIECES[p]
        here = x if h == 0 else z
        rows = pl.ds(q, n)
        for e in range(2):
            target = (here + 2 * e + 3) % SIDE
            raw_copies[2 * p + e].wait_recv()
            mine = own_codes(h, target, 2 * e, b, r0, n)
            other = near_codes(raw, (e, slice(None), rows), h, e, target, 2 * e, b, r0, n)
            for i in range(8):
                total = (mine[i] + other[i]).astype(jnp.bfloat16)
                first_send[e, pl.ds(2 * e, 2), rows, lanes(i)] = total.reshape(2, n, LANES)
            if p not in LEAVES:
                mine = own_codes(h, target, 2 * (1 - e), b, r0, n)
                for i in range(8):
                    first_send[e, pl.ds(2 * (1 - e), 2), rows, lanes(i)] = mine[i].astype(jnp.bfloat16).reshape(2, n, LANES)
            sent = pl.ds(2 * e, 2) if p in LEAVES else slice(None)
            copy = pltpu.make_async_remote_copy(
                first_send.at[e, sent, rows, :], first_recv.at[e, sent, rows, :],
                first_ss.at[2 * p + e], first_rs.at[2 * p + e],
                device_id=neighbour(h, 2 * e - 1), device_id_type=MESH)
            copy.start()
            first_copies[2 * p + e] = copy

    mid_copies, last_copies = {}, {}

    def combine(p):
        h, b, r0, n, q = PIECES[p]
        here, there = (x, z) if h == 0 else (z, x)
        rows = pl.ds(q, n)
        for e in range(2):
            first_copies[2 * p + e].wait_recv()

        def fill(half):
            pair = pl.ds(2 * half, 2)
            mine = own_codes(h, here, 2 * half, b, r0, n)
            if p in LEAVES:
                mine_too = near_codes(leaf, (1 - half, slice(None), pl.ds(LEAVES[p], n)), h, 1 - half, here, 2 * half, b, r0, n)
            for i in range(8):
                total = mine[i]
                if p in LEAVES:
                    total += mine_too[i] + first_recv[half, pair, rows, lanes(i)].astype(jnp.float32).reshape(2 * n, LANES)
                else:
                    for e in range(2):
                        total += first_recv[e, pair, rows, lanes(i)].astype(jnp.float32).reshape(2 * n, LANES)
                partial[pair, rows, lanes(i)] = total.astype(jnp.int32).astype(jnp.int16).reshape(2, n, LANES)

        def send():
            for e in range(2):
                copy = pltpu.make_async_remote_copy(
                    partial.at[(there + 2) % SIDE, rows, pl.ds(512 * e, 512)], second_raw.at[e, rows, :],
                    mid_ss.at[2 * p + e], mid_rs.at[2 * p + e],
                    device_id=neighbour(1 - h, 2 * e - 1), device_id_type=MESH)
                copy.start()
                mid_copies[2 * p + e] = copy

        if p in LEAVES:
            for e in range(2):
                leaf_copies[2 * p + e].wait_recv()
            fill(0)
            fill(1)
            send()
        else:
            opposite = (there + 2) % SIDE // 2
            fill(opposite)
            send()
            fill(1 - opposite)

    def forward(p):
        h, b, r0, n, q = PIECES[p]
        there = z if h == 0 else x
        rows = pl.ds(q, n)
        for e in range(2):
            mid_copies[2 * p + e].wait_recv()
            j = (there + 2 * e + 3) % SIDE
            plain, summed = pl.ds(512 * (1 - e), 512), pl.ds(512 * e, 512)
            second_send[e, rows, plain] = partial[j, rows, plain]
            total = partial[j, rows, summed].astype(jnp.int32) + second_raw[e, rows, :].astype(jnp.int32)
            second_send[e, rows, summed] = total.astype(jnp.int16)
            copy = pltpu.make_async_remote_copy(
                second_send.at[e, rows, :], second_recv.at[e, rows, :],
                last_ss.at[2 * p + e], last_rs.at[2 * p + e],
                device_id=neighbour(1 - h, 2 * e - 1), device_id_type=MESH)
            copy.start()
            last_copies[2 * p + e] = copy

    def decode(p):
        h, b, r0, n, q = PIECES[p]
        there = z if h == 0 else x
        rows = pl.ds(q, n)
        for e in range(2):
            last_copies[2 * p + e].wait_recv()
        parts = []
        for k in range(SIDE):
            cols = pl.ds(k * SUB, SUB)
            total = partial[there, rows, cols].astype(jnp.int32)
            for e in range(2):
                total += second_recv[e, rows, cols].astype(jnp.int32)
            total = total.astype(jnp.float32)
            high = total.astype(jnp.bfloat16)
            low = (total - high.astype(jnp.float32)).astype(jnp.bfloat16)
            parts.append(jnp.dot(high, table[...], preferred_element_type=jnp.float32)
                         + jnp.dot(low, table[...], preferred_element_type=jnp.float32))
        values = butterfly(parts)
        factor = peak_ref[1, 0:1, :]
        for i in range(8):
            col = b * BLOCK + i * LANES
            flips = (1 - 2 * sign_ref[:, col:col + LANES]).astype(jnp.float32)
            value = values[i // 2][:, (i % 2) * LANES:(i % 2 + 1) * LANES]
            out_ref[r0:r0 + n, col:col + LANES] = (value * factor * flips).astype(jnp.bfloat16)

    count = len(PIECES) // 2
    tasks = ((first, 0), (combine, 2), (forward, 3), (decode, 4))
    for step in range(count + 4):
        for task, lag in tasks:
            for p in (2 * (step - lag), 2 * (step - lag) + 1):
                if 0 <= p < len(PIECES):
                    task(p)
    for copies in (raw_copies, leaf_copies, first_copies, mid_copies, last_copies):
        for copy in copies.values():
            copy.wait_send()
    for copy in near_copies + peak_copies:
        copy.wait_send()


def local(gradients, dither, sign_bits):
    row_count, col_count = gradients.shape[1:]
    grad = gradients.reshape(SIDE, SIDE, row_count // 16, col_count)
    vmem, dma = pltpu.VMEM, pltpu.SemaphoreType.DMA
    pieces = 2 * len(PIECES)
    return pl.pallas_call(
        kernel,
        out_shape=jax.ShapeDtypeStruct((row_count // 16, col_count), jnp.bfloat16),
        in_specs=[pl.BlockSpec(memory_space=pltpu.HBM)] * 3,
        out_specs=pl.BlockSpec(memory_space=pltpu.VMEM),
        scratch_shapes=[
            vmem((1, row_count), jnp.int32),
            vmem((1, col_count), jnp.int32),
            vmem((SIDE, SIDE, 144, col_count), jnp.bfloat16),
            vmem((3, SIDE, SUB, SUB), jnp.bfloat16),
            vmem((SUB, SUB), jnp.bfloat16),
            vmem((SIDE, SIDE, 144, LANES), jnp.float32),
            vmem((4, 1, row_count), jnp.int32),
            vmem((4, SIDE, SIDE, 144, LANES), jnp.float32),
            vmem((24, LANES), jnp.float32),
            vmem((1, BLOCK), jnp.float32),
            vmem((3, 8, LANES), jnp.float32),
            vmem((13, 8, LANES), jnp.float32),
            vmem((2, 8, LANES), jnp.float32),
            vmem((2, 2, ROWS, BLOCK), jnp.bfloat16),
            vmem((2, 2, LEAF_ROWS, BLOCK), jnp.bfloat16),
            vmem((2, SIDE, ROWS, BLOCK), jnp.bfloat16),
            vmem((2, SIDE, ROWS, BLOCK), jnp.bfloat16),
            vmem((SIDE, ROWS, BLOCK), jnp.int16),
            vmem((2, ROWS, 512), jnp.int16),
            vmem((2, ROWS, BLOCK), jnp.int16),
            vmem((2, ROWS, BLOCK), jnp.int16),
            dma((2,)), dma((16,)), dma((4,)), dma((4,)), dma((13,)), dma((13,)), dma((pieces,)), dma((pieces,)),
            dma((4,)), dma((4,)), dma((pieces,)), dma((pieces,)), dma((pieces,)), dma((pieces,)), dma((pieces,)), dma((pieces,)),
        ],
        compiler_params=pltpu.CompilerParams(collective_id=0, has_side_effects=True, vmem_limit_bytes=50 * 2**20),
    )(grad, dither, sign_bits.reshape(1, col_count))


def solution(mesh):
    return jax.shard_map(
        local,
        mesh=mesh,
        in_specs=(P("dp", None, "tensor"), P("dp", None), P("tensor")),
        out_specs=P("dp", "tensor"),
        check_vma=False,
    )
```

```python
import functools

import jax
import jax.numpy as jnp
from jax import lax
from jax.experimental import pallas as pl
from jax.experimental.pallas import tpu as pltpu
from jax.sharding import PartitionSpec as P

BLOCK = 1024
LEVELS = 127
SIDE = 4
SUB = 256
LANES = 128
MESH = pl.DeviceIdType.MESH

PIECES = (
    (0, 0, 0, 48, 0), (1, 2, 0, 48, 224),
    (0, 0, 48, 48, 48), (1, 2, 48, 48, 272),
    (0, 0, 96, 48, 96), (1, 2, 96, 48, 320),
    (0, 1, 0, 48, 144), (1, 1, 80, 32, 368),
    (0, 1, 48, 32, 192), (1, 1, 112, 32, 400),
)
ROWS = 432
ORDER = ((0, 0), (0, 1), (0, 2), (0, 3), (1, 0), (0, 4), (1, 1), (1, 2), (2, 0), (1, 3), (2, 1), (1, 4), (2, 2), (3, 0), (2, 3), (2, 4), (3, 1), (3, 2), (3, 3), (3, 4))
RAW_EARLY = (0, 1, 2, 3)
RAW_LATE = (4, 5, 6, 7, 8, 9)
LEAVES = {0: 0, 1: 48, 2: 96, 3: 144}
LEAF_ROWS = 192


def butterfly(parts):
    a, b = parts[0] + parts[1], parts[0] - parts[1]
    c, d = parts[2] + parts[3], parts[2] - parts[3]
    return [a + c, b + d, a - c, b - d]


def kernel(grad, small_in, out_ref, dither_ref, sign_ref, held, weights, table, own_dither, near_raw, near_dither, rows_of, ramp, peak_send,
           peak_recv, peak_all, peak_ref, raw, leaf, first_send, first_recv, partial, second_raw, second_send, second_recv,
           small_sem, load_sem, near_ss, near_rs, peak_ss, peak_rs, raw_ss, raw_rs, leaf_ss, leaf_rs, first_ss, first_rs, mid_ss, mid_rs, last_ss, last_rs):
    dp, tensor = lax.axis_index("dp"), lax.axis_index("tensor")
    x, z = dp // SIDE, dp % SIDE

    def lanes(i):
        return slice(i * LANES, (i + 1) * LANES)

    core = tensor % 2
    turns = (core, 1 - core)

    def place(step_x, step_z, step_t):
        return ((x + step_x + SIDE) % SIDE * SIDE + (z + step_z + SIDE) % SIDE, (tensor + step_t + 8) % 8)

    def neighbour(axis, step):
        return place(step * (1 - axis), step * axis, 0)

    def spots(h):
        return x + turns[h] * (z - x), z + turns[h] * (x - z)

    def target_of(h, here, there):
        return here * (SIDE - 3 * turns[h]) + there * (1 + 3 * turns[h])

    stages = (
        [place(i, 0, 0) for i in range(1, SIDE)],
        [place(0, 0, 2 * i) for i in range(1, SIDE)],
        [place(0, i, 2) for i in range(1, SIDE)],
    )
    partner = (dp, tensor + 1 - 2 * core)
    next_to = [place(1, 0, 0), place(-1, 0, 0), place(0, 1, 0), place(0, -1, 0)]
    further = [place(2, 0, 0)] + stages[1] + [place(0, -i, -2) for i in range(1, SIDE)] + [partner]
    barrier = pltpu.get_barrier_semaphore()
    for peer in next_to:
        pl.semaphore_signal(barrier, inc=1, device_id=peer, device_id_type=MESH)

    @pl.when(core == 0)
    def _():
        for peer in further:
            pl.semaphore_signal(barrier, inc=1, device_id=peer, device_id_type=MESH)


    split = dither_ref.shape[1]
    small = [pltpu.make_async_copy(small_in.at[:, pl.ds(0, split)], dither_ref, small_sem.at[0]),
             pltpu.make_async_copy(small_in.at[:, pl.ds(split, sign_ref.shape[1])], sign_ref, small_sem.at[1])]
    for copy in small:
        copy.start()
    def load(c):
        return pltpu.make_async_copy(grad.at[c], held.at[c], load_sem.at[c])

    def start_load(c, carry):
        load(c).start()
        return carry

    pl.semaphore_wait(barrier, 11 - 6 * core)

    def row_copies(p, here, j, buffer, first, e, send_sem, recv_sem):
        h, b, r0, n, q = PIECES[p]
        copies = []
        for jj in range(2):
            i = 4 * p + 2 * e + jj
            copies.append(pltpu.make_async_remote_copy(
                grad.at[target_of(h, here, j + jj), pl.ds(r0, n), pl.ds(b * BLOCK, BLOCK)],
                buffer.at[e, jj, pl.ds(first, n), :], send_sem.at[i], recv_sem.at[i],
                device_id=neighbour(turns[h], 2 * e - 1), device_id_type=MESH))
        return copies

    def raw_copies(p, e):
        far = (spots(PIECES[p][0])[0] + 2) % SIDE
        return row_copies(p, far, 2 * e, raw, PIECES[p][4], e, raw_ss, raw_rs)

    def leaf_copies(p, e):
        target = (spots(PIECES[p][0])[0] + 2 * e + 3) % SIDE
        return row_copies(p, target, 2 * (1 - e), leaf, LEAVES[p], e, leaf_ss, leaf_rs)

    def send_raw(p):
        for e in range(2):
            for copy in raw_copies(p, e):
                copy.start()

    def send_late():
        for p in RAW_LATE:
            send_raw(p)
        for p in LEAVES:
            for e in range(2):
                for copy in leaf_copies(p, e):
                    copy.start()

    for p in RAW_EARLY[:2]:
        send_raw(p)
    lax.fori_loop(0, SIDE * SIDE, start_load, 0)
    small[0].wait()
    near_copies = []
    for i in range(4):
        copy = pltpu.make_async_remote_copy(
            dither_ref, near_raw.at[i], near_ss.at[i], near_rs.at[i],
            device_id=neighbour(turns[i // 2], 2 * (i % 2) - 1), device_id_type=MESH)
        copy.start()
        near_copies.append(copy)

    for p in RAW_EARLY[2:]:
        send_raw(p)
    pl.when(core == 1)(send_late)

    bits = lax.broadcasted_iota(jnp.int32, (SUB, SUB), 0) & lax.broadcasted_iota(jnp.int32, (SUB, SUB), 1)
    bits = bits ^ (bits >> 4)
    bits = bits ^ (bits >> 2)
    bits = bits ^ (bits >> 1)
    base = (1 - 2 * (bits & 1)).astype(jnp.float32).astype(jnp.bfloat16)
    table[...] = base
    small[1].wait()
    diagonal = lax.broadcasted_iota(jnp.int32, (SUB, SUB), 0) == lax.broadcasted_iota(jnp.int32, (SUB, SUB), 1)
    for i in range(12):
        flips = (1 - 2 * sign_ref[:, i * SUB:(i + 1) * SUB]).astype(jnp.float32)
        scaled = jnp.where(diagonal, flips, 0.0).astype(jnp.bfloat16)
        weights[i // SIDE, i % SIDE] = jnp.dot(scaled, base, preferred_element_type=jnp.float32).astype(jnp.bfloat16)
    column = lax.broadcasted_iota(jnp.int32, (1, BLOCK), 1)
    ramp[...] = (((7919 * column) & (BLOCK - 1)).astype(jnp.float32) + 0.5) * (1.0 / BLOCK)

    def parts_of(views, b):
        parts = []
        for k in range(SIDE):
            values = jnp.concatenate([view[:, k * SUB:(k + 1) * SUB] for view in views], axis=0)
            parts.append(jnp.dot(values, weights[b, k], preferred_element_type=jnp.float32))
        return parts

    def peak_of(c, top):
        load(2 * c).wait()
        load(2 * c + 1).wait()
        for b in range(3):
            m = parts_of([held.at[2 * c + i, :, pl.ds(b * BLOCK, BLOCK)] for i in range(2)], b)
            even = jnp.abs(m[0] + m[1]) + jnp.abs(m[2] + m[3])
            odd = jnp.abs(m[0] - m[1]) + jnp.abs(m[2] - m[3])
            both = jnp.maximum(even, odd)
            both = jnp.maximum(both[:, :LANES], both[:, LANES:])
            top = jnp.maximum(top, jnp.max(both.reshape(36, 8, LANES), axis=0))
        return top

    top = lax.fori_loop(0, SIDE * 2, peak_of, jnp.zeros((8, LANES), jnp.float32))

    def spread(source, target):
        for i in range(18):
            rows_of[i:i + 1, :] = source[:, lanes(i)].astype(jnp.float32) * (1.0 / BLOCK)
        turned = jnp.transpose(rows_of[...], (1, 0))
        for i in range(18):
            spread_rows = jnp.broadcast_to(turned[:, i:i + 1], (LANES, LANES))
            start = i * LANES
            while start < (i + 1) * LANES:
                c, r = start // 144, start % 144
                n = min(144 - r, (i + 1) * LANES - start)
                target[c, r:r + n, :] = spread_rows[start - i * LANES:start - i * LANES + n]
                start += n

    def peak_copy(source, target, i, peer):
        return pltpu.make_async_remote_copy(
            peak_send.at[source], target, peak_ss.at[i], peak_rs.at[i], device_id=peer, device_id_type=MESH)

    def from_core_1():
        return peak_copy(0, peak_recv.at[0], 0, partner)

    def to_core_1():
        return peak_copy(4, peak_all, 10, partner)

    def stage_copies(s):
        return [peak_copy(1 + s, peak_recv.at[1 + 3 * s + i], 1 + 3 * s + i, peer) for i, peer in enumerate(stages[s])]

    def start_stage(s, value):
        peak_send[1 + s] = value
        for copy in stage_copies(s):
            copy.start()

    def end_stage(s):
        value = peak_send[1 + s]
        for i, copy in enumerate(stage_copies(s)):
            copy.wait_recv()
            value = jnp.maximum(value, peak_recv[1 + 3 * s + i])
        return value

    peak_send[0] = top

    @pl.when(core == 1)
    def _():
        from_core_1().start()

    @pl.when(core == 0)
    def _():
        from_core_1().wait_recv()
        start_stage(0, jnp.maximum(peak_send[0], peak_recv[0]))
        send_late()

    spread(dither_ref, own_dither)
    for i in range(4):
        near_copies[i].wait_recv()
        spread(near_raw.at[i], near_dither.at[i])

    @pl.when(core == 0)
    def _():
        start_stage(1, end_stage(0))
        start_stage(2, end_stage(1))
        value = end_stage(2)
        peak_send[4] = value
        to_core_1().start()
        peak_all[...] = value

    @pl.when(core == 1)
    def _():
        to_core_1().wait_recv()

    top = peak_all[...]
    top = jnp.max(jnp.max(top, axis=1, keepdims=True), axis=0, keepdims=True)
    peak = jnp.broadcast_to(top, (8, LANES))
    peak_ref[0] = LEVELS / peak
    peak_ref[1] = peak / (LEVELS * 16 * BLOCK)

    def codes(views, b, offsets):
        values = butterfly(parts_of(views, b))
        offsets = jnp.concatenate(offsets, axis=0)
        scale = peak_ref[0, 0:1, :]
        result = []
        for i in range(8):
            shift = offsets + ramp[:, lanes(i)]
            shift = shift - jnp.floor(shift)
            value = values[i // 2][:, (i % 2) * LANES:(i % 2 + 1) * LANES]
            result.append(jnp.floor(value * scale + shift))
        return result

    def own_codes(h, here, j, b, r0, n):
        targets = [target_of(h, here, j + jj) for jj in range(2)]
        rows = pl.ds(r0, n)
        return codes([held.at[c, rows, pl.ds(b * BLOCK, BLOCK)] for c in targets], b, [own_dither[c, rows, :] for c in targets])

    def near_codes(buffer, first, h, e, here, j, b, r0, n):
        targets = [target_of(h, here, j + jj) for jj in range(2)]
        views = [buffer.at[e, jj, pl.ds(first, n), :] for jj in range(2)]
        return codes(views, b, [near_dither[2 * h + e, c, pl.ds(r0, n), :] for c in targets])

    first_copies = {}

    def first(p):
        h, b, r0, n, q = PIECES[p]
        here = spots(h)[0]
        rows = pl.ds(q, n)
        for e in range(2):
            target = (here + 2 * e + 3) % SIDE
            for copy in raw_copies(p, e):
                copy.wait_recv()
            mine = own_codes(h, target, 2 * e, b, r0, n)
            other = near_codes(raw, q, h, e, target, 2 * e, b, r0, n)
            for i in range(8):
                total = (mine[i] + other[i]).astype(jnp.bfloat16)
                first_send[e, pl.ds(2 * e, 2), rows, lanes(i)] = total.reshape(2, n, LANES)
            if p not in LEAVES:
                mine = own_codes(h, target, 2 * (1 - e), b, r0, n)
                for i in range(8):
                    first_send[e, pl.ds(2 * (1 - e), 2), rows, lanes(i)] = mine[i].astype(jnp.bfloat16).reshape(2, n, LANES)
            sent = pl.ds(2 * e, 2) if p in LEAVES else slice(None)
            copy = pltpu.make_async_remote_copy(
                first_send.at[e, sent, rows, :], first_recv.at[e, sent, rows, :],
                first_ss.at[2 * p + e], first_rs.at[2 * p + e],
                device_id=neighbour(turns[h], 2 * e - 1), device_id_type=MESH)
            copy.start()
            first_copies[2 * p + e] = copy

    mid_copies, last_copies = {}, {}

    def combine(p):
        h, b, r0, n, q = PIECES[p]
        here, there = spots(h)
        rows = pl.ds(q, n)
        for e in range(2):
            first_copies[2 * p + e].wait_recv()

        def fill(half):
            pair = pl.ds(2 * half, 2)
            mine = own_codes(h, here, 2 * half, b, r0, n)
            if p in LEAVES:
                mine_too = near_codes(leaf, LEAVES[p], h, 1 - half, here, 2 * half, b, r0, n)
            for i in range(8):
                total = mine[i]
                if p in LEAVES:
                    total += mine_too[i] + first_recv[half, pair, rows, lanes(i)].astype(jnp.float32).reshape(2 * n, LANES)
                else:
                    for e in range(2):
                        total += first_recv[e, pair, rows, lanes(i)].astype(jnp.float32).reshape(2 * n, LANES)
                partial[pair, rows, lanes(i)] = total.astype(jnp.int32).astype(jnp.int16).reshape(2, n, LANES)

        def send():
            for e in range(2):
                copy = pltpu.make_async_remote_copy(
                    partial.at[(there + 2) % SIDE, rows, pl.ds(512 * e, 512)], second_raw.at[e, rows, :],
                    mid_ss.at[2 * p + e], mid_rs.at[2 * p + e],
                    device_id=neighbour(1 - turns[h], 2 * e - 1), device_id_type=MESH)
                copy.start()
                mid_copies[2 * p + e] = copy

        if p in LEAVES:
            for e in range(2):
                for copy in leaf_copies(p, e):
                    copy.wait_recv()
            fill(0)
            fill(1)
            send()
        else:
            opposite = (there + 2) % SIDE // 2
            fill(opposite)
            send()
            fill(1 - opposite)

    def forward(p):
        h, b, r0, n, q = PIECES[p]
        there = spots(h)[1]
        rows = pl.ds(q, n)
        for e in range(2):
            mid_copies[2 * p + e].wait_recv()
            j = (there + 2 * e + 3) % SIDE
            plain, summed = pl.ds(512 * (1 - e), 512), pl.ds(512 * e, 512)
            second_send[e, rows, plain] = partial[j, rows, plain]
            total = partial[j, rows, summed].astype(jnp.int32) + second_raw[e, rows, :].astype(jnp.int32)
            second_send[e, rows, summed] = total.astype(jnp.int16)
            copy = pltpu.make_async_remote_copy(
                second_send.at[e, rows, :], second_recv.at[e, rows, :],
                last_ss.at[2 * p + e], last_rs.at[2 * p + e],
                device_id=neighbour(1 - turns[h], 2 * e - 1), device_id_type=MESH)
            copy.start()
            last_copies[2 * p + e] = copy

    def decode(p):
        h, b, r0, n, q = PIECES[p]
        there = spots(h)[1]
        rows = pl.ds(q, n)
        for e in range(2):
            last_copies[2 * p + e].wait_recv()
        parts = []
        for k in range(SIDE):
            cols = pl.ds(k * SUB, SUB)
            total = partial[there, rows, cols].astype(jnp.int32)
            for e in range(2):
                total += second_recv[e, rows, cols].astype(jnp.int32)
            total = total.astype(jnp.float32)
            high = total.astype(jnp.bfloat16)
            low = (total - high.astype(jnp.float32)).astype(jnp.bfloat16)
            parts.append(jnp.dot(high, table[...], preferred_element_type=jnp.float32)
                         + jnp.dot(low, table[...], preferred_element_type=jnp.float32))
        values = butterfly(parts)
        factor = peak_ref[1, 0:1, :]
        for i in range(8):
            col = b * BLOCK + i * LANES
            flips = (1 - 2 * sign_ref[:, col:col + LANES]).astype(jnp.float32)
            value = values[i // 2][:, (i % 2) * LANES:(i % 2 + 1) * LANES]
            out_ref[r0:r0 + n, col:col + LANES] = (value * factor * flips).astype(jnp.bfloat16)

    tasks = (first, combine, forward, decode)
    for kind, step in ORDER:
        for p in (2 * step, 2 * step + 1):
            if p < len(PIECES):
                tasks[kind](p)
    for copies in (first_copies, mid_copies, last_copies):
        for copy in copies.values():
            copy.wait_send()
    for e in range(2):
        for copy in sum([raw_copies(p, e) for p in range(len(PIECES))], []) + sum([leaf_copies(p, e) for p in LEAVES], []):
            copy.wait_send()
    for copy in near_copies:
        copy.wait_send()

    @pl.when(core == 0)
    def _():
        for s in range(3):
            for copy in stage_copies(s):
                copy.wait_send()
        to_core_1().wait_send()

    @pl.when(core == 1)
    def _():
        from_core_1().wait_send()


def local(gradients, dither, sign_bits):
    row_count, col_count = gradients.shape[1:]
    grad = gradients.reshape(16, row_count // 16, col_count)
    vmem, dma = pltpu.VMEM, pltpu.SemaphoreType.DMA
    pieces = 2 * len(PIECES)
    return pl.pallas_call(
        kernel,
        out_shape=jax.ShapeDtypeStruct((row_count // 16, col_count), jnp.bfloat16),
        in_specs=[pl.BlockSpec(memory_space=pl.ANY)] * 2,
        out_specs=pl.BlockSpec(memory_space=pltpu.VMEM),
        scratch_shapes=[
            vmem((1, row_count), jnp.int32),
            vmem((1, col_count), jnp.int32),
            vmem((16, 144, col_count), jnp.bfloat16),
            vmem((3, SIDE, SUB, SUB), jnp.bfloat16),
            vmem((SUB, SUB), jnp.bfloat16),
            vmem((16, 144, LANES), jnp.float32),
            vmem((4, 1, row_count), jnp.int32),
            vmem((4, 16, 144, LANES), jnp.float32),
            vmem((24, LANES), jnp.float32),
            vmem((1, BLOCK), jnp.float32),
            vmem((5, 8, LANES), jnp.float32),
            vmem((10, 8, LANES), jnp.float32),
            vmem((8, LANES), jnp.float32),
            vmem((2, 8, LANES), jnp.float32),
            vmem((2, 2, ROWS, BLOCK), jnp.bfloat16),
            vmem((2, 2, LEAF_ROWS, BLOCK), jnp.bfloat16),
            vmem((2, SIDE, ROWS, BLOCK), jnp.bfloat16),
            vmem((2, SIDE, ROWS, BLOCK), jnp.bfloat16),
            vmem((SIDE, ROWS, BLOCK), jnp.int16),
            vmem((2, ROWS, 512), jnp.int16),
            vmem((2, ROWS, BLOCK), jnp.int16),
            vmem((2, ROWS, BLOCK), jnp.int16),
            dma((2,)), dma((16,)), dma((4,)), dma((4,)), dma((11,)), dma((11,)), dma((2 * pieces,)), dma((2 * pieces,)),
            dma((4 * len(LEAVES),)), dma((4 * len(LEAVES),)), dma((pieces,)), dma((pieces,)), dma((pieces,)), dma((pieces,)), dma((pieces,)), dma((pieces,)),
        ],
        compiler_params=pltpu.CompilerParams(collective_id=0, has_side_effects=True, vmem_limit_bytes=50 * 2**20),
    )(grad, jnp.concatenate([dither, sign_bits.reshape(1, col_count)], axis=1))


def solution(mesh):
    return jax.shard_map(
        local,
        mesh=mesh,
        in_specs=(P("dp", None, "tensor"), P("dp", None), P("tensor")),
        out_specs=P("dp", "tensor"),
        check_vma=False,
    )
```

```python
import functools

import jax
import jax.numpy as jnp
from jax import lax
from jax.experimental import pallas as pl
from jax.experimental.pallas import tpu as pltpu
from jax.sharding import PartitionSpec as P

BLOCK = 1024
LEVELS = 127
SIDE = 4
SUB = 256
LANES = 128
MESH = pl.DeviceIdType.MESH

PIECES = (
    (0, 0, 0, 48, 0), (1, 2, 0, 48, 224),
    (0, 0, 48, 48, 48), (1, 2, 48, 48, 272),
    (0, 0, 96, 48, 96), (1, 2, 96, 48, 320),
    (0, 1, 0, 48, 144), (1, 1, 80, 32, 368),
    (0, 1, 48, 32, 192), (1, 1, 112, 32, 400),
)
ROWS = 432
ORDER = ((0, 0), (0, 1), (0, 2), (0, 3), (1, 0), (0, 4), (1, 1), (1, 2), (2, 0), (1, 3), (2, 1), (1, 4), (2, 2), (3, 0), (2, 3), (2, 4), (3, 1), (3, 2), (3, 3), (3, 4))
RAW_EARLY = (0, 1, 2, 3)
RAW_LATE = (4, 5, 6, 7, 8, 9)
LEAVES = {0: 0, 1: 48, 2: 96, 3: 144}
LEAF_ROWS = 192


def butterfly(parts):
    a, b = parts[0] + parts[1], parts[0] - parts[1]
    c, d = parts[2] + parts[3], parts[2] - parts[3]
    return [a + c, b + d, a - c, b - d]


def kernel(grad, small_in, out_ref, dither_ref, sign_ref, held, weights, table, own_dither, near_raw, near_dither, own_rows, ramp, peak_send,
           peak_recv, peak_all, peak_ref, raw, leaf, first_send, first_recv, partial, second_raw, second_send, second_recv,
           small_sem, load_sem, near_ss, near_rs, peak_ss, peak_rs, raw_ss, raw_rs, leaf_ss, leaf_rs, first_ss, first_rs, mid_ss, mid_rs, last_ss, last_rs):
    dp, tensor = lax.axis_index("dp"), lax.axis_index("tensor")
    x, z = dp // SIDE, dp % SIDE

    def lanes(i):
        return slice(i * LANES, (i + 1) * LANES)

    core = tensor % 2
    turns = (core, 1 - core)

    def place(step_x, step_z, step_t):
        return ((x + step_x + SIDE) % SIDE * SIDE + (z + step_z + SIDE) % SIDE, (tensor + step_t + 8) % 8)

    def neighbour(axis, step):
        return place(step * (1 - axis), step * axis, 0)

    def spots(h):
        return x + turns[h] * (z - x), z + turns[h] * (x - z)

    def target_of(h, here, there):
        return here * (SIDE - 3 * turns[h]) + there * (1 + 3 * turns[h])

    stages = (
        [place(i, 0, 0) for i in range(1, SIDE)],
        [place(0, 0, 2 * i) for i in range(1, SIDE)],
        [place(0, i, 2) for i in range(1, SIDE)],
    )
    partner = (dp, tensor + 1 - 2 * core)
    next_to = [place(1, 0, 0), place(-1, 0, 0), place(0, 1, 0), place(0, -1, 0)]
    further = [place(2, 0, 0)] + stages[1] + [place(0, -i, -2) for i in range(1, SIDE)] + [partner]
    barrier = pltpu.get_barrier_semaphore()
    for peer in next_to:
        pl.semaphore_signal(barrier, inc=1, device_id=peer, device_id_type=MESH)

    @pl.when(core == 0)
    def _():
        for peer in further:
            pl.semaphore_signal(barrier, inc=1, device_id=peer, device_id_type=MESH)


    split = dither_ref.shape[1]
    small = [pltpu.make_async_copy(small_in.at[:, pl.ds(0, split)], dither_ref, small_sem.at[0]),
             pltpu.make_async_copy(small_in.at[:, pl.ds(split, sign_ref.shape[1])], sign_ref, small_sem.at[1])]
    for copy in small:
        copy.start()
    def load(c):
        return pltpu.make_async_copy(grad.at[c], held.at[c], load_sem.at[c])

    def start_load(c, carry):
        load(c).start()
        return carry

    pl.semaphore_wait(barrier, 11 - 6 * core)

    def row_copies(p, here, j, buffer, first, e, send_sem, recv_sem):
        h, b, r0, n, q = PIECES[p]
        copies = []
        for jj in range(2):
            i = 4 * p + 2 * e + jj
            copies.append(pltpu.make_async_remote_copy(
                grad.at[target_of(h, here, j + jj), pl.ds(r0, n), pl.ds(b * BLOCK, BLOCK)],
                buffer.at[e, jj, pl.ds(first, n), :], send_sem.at[i], recv_sem.at[i],
                device_id=neighbour(turns[h], 2 * e - 1), device_id_type=MESH))
        return copies

    def raw_copies(p, e):
        far = (spots(PIECES[p][0])[0] + 2) % SIDE
        return row_copies(p, far, 2 * e, raw, PIECES[p][4], e, raw_ss, raw_rs)

    def leaf_copies(p, e):
        target = (spots(PIECES[p][0])[0] + 2 * e + 3) % SIDE
        return row_copies(p, target, 2 * (1 - e), leaf, LEAVES[p], e, leaf_ss, leaf_rs)

    def send_raw(p):
        for e in range(2):
            for copy in raw_copies(p, e):
                copy.start()

    def send_late():
        for p in RAW_LATE:
            send_raw(p)
        for p in LEAVES:
            for e in range(2):
                for copy in leaf_copies(p, e):
                    copy.start()

    for p in RAW_EARLY[:2]:
        send_raw(p)
    lax.fori_loop(0, SIDE * SIDE, start_load, 0)
    small[0].wait()
    own_rows[...] = jnp.zeros_like(own_rows)
    for i in range(18):
        own_rows[i:i + 1, :] = dither_ref[:, lanes(i)]
    near_copies = []
    for i in range(4):
        copy = pltpu.make_async_remote_copy(
            own_rows, near_raw.at[i], near_ss.at[i], near_rs.at[i],
            device_id=neighbour(turns[i // 2], 2 * (i % 2) - 1), device_id_type=MESH)
        copy.start()
        near_copies.append(copy)

    for p in RAW_EARLY[2:]:
        send_raw(p)
    pl.when(core == 1)(send_late)

    bits = lax.broadcasted_iota(jnp.int32, (SUB, SUB), 0) & lax.broadcasted_iota(jnp.int32, (SUB, SUB), 1)
    bits = bits ^ (bits >> 4)
    bits = bits ^ (bits >> 2)
    bits = bits ^ (bits >> 1)
    base = (1 - 2 * (bits & 1)).astype(jnp.float32).astype(jnp.bfloat16)
    table[...] = base
    small[1].wait()
    diagonal = lax.broadcasted_iota(jnp.int32, (SUB, SUB), 0) == lax.broadcasted_iota(jnp.int32, (SUB, SUB), 1)
    for i in range(12):
        flips = (1 - 2 * sign_ref[:, i * SUB:(i + 1) * SUB]).astype(jnp.float32)
        scaled = jnp.where(diagonal, flips, 0.0).astype(jnp.bfloat16)
        weights[i // SIDE, i % SIDE] = jnp.dot(scaled, base, preferred_element_type=jnp.float32).astype(jnp.bfloat16)
    column = lax.broadcasted_iota(jnp.int32, (1, BLOCK), 1)
    ramp[...] = (((7919 * column) & (BLOCK - 1)).astype(jnp.float32) + 0.5) * (1.0 / BLOCK)

    def parts_of(views, b):
        parts = []
        for k in range(SIDE):
            values = jnp.concatenate([view[:, k * SUB:(k + 1) * SUB] for view in views], axis=0)
            parts.append(jnp.dot(values, weights[b, k], preferred_element_type=jnp.float32))
        return parts

    def peak_of(c, top):
        load(2 * c).wait()
        load(2 * c + 1).wait()
        for b in range(3):
            m = parts_of([held.at[2 * c + i, :, pl.ds(b * BLOCK, BLOCK)] for i in range(2)], b)
            even = jnp.abs(m[0] + m[1]) + jnp.abs(m[2] + m[3])
            odd = jnp.abs(m[0] - m[1]) + jnp.abs(m[2] - m[3])
            both = jnp.maximum(even, odd)
            both = jnp.maximum(both[:, :LANES], both[:, LANES:])
            top = jnp.maximum(top, jnp.max(both.reshape(36, 8, LANES), axis=0))
        return top

    top = lax.fori_loop(0, SIDE * 2, peak_of, jnp.zeros((8, LANES), jnp.float32))

    def spread(source, target):
        turned = jnp.transpose(source[...].astype(jnp.float32) * (1.0 / BLOCK), (1, 0))
        for i in range(18):
            spread_rows = jnp.broadcast_to(turned[:, i:i + 1], (LANES, LANES))
            start = i * LANES
            while start < (i + 1) * LANES:
                c, r = start // 144, start % 144
                n = min(144 - r, (i + 1) * LANES - start)
                target[c, r:r + n, :] = spread_rows[start - i * LANES:start - i * LANES + n]
                start += n

    def peak_copy(source, target, i, peer):
        return pltpu.make_async_remote_copy(
            peak_send.at[source], target, peak_ss.at[i], peak_rs.at[i], device_id=peer, device_id_type=MESH)

    def from_core_1():
        return peak_copy(0, peak_recv.at[0], 0, partner)

    def to_core_1():
        return peak_copy(4, peak_all, 10, partner)

    def stage_copies(s):
        return [peak_copy(1 + s, peak_recv.at[1 + 3 * s + i], 1 + 3 * s + i, peer) for i, peer in enumerate(stages[s])]

    def start_stage(s, value):
        peak_send[1 + s] = value
        for copy in stage_copies(s):
            copy.start()

    def end_stage(s):
        value = peak_send[1 + s]
        for i, copy in enumerate(stage_copies(s)):
            copy.wait_recv()
            value = jnp.maximum(value, peak_recv[1 + 3 * s + i])
        return value

    peak_send[0] = top

    @pl.when(core == 1)
    def _():
        from_core_1().start()

    @pl.when(core == 0)
    def _():
        from_core_1().wait_recv()
        start_stage(0, jnp.maximum(peak_send[0], peak_recv[0]))
        send_late()

    spread(own_rows, own_dither)
    for i in range(4):
        near_copies[i].wait_recv()
        spread(near_raw.at[i], near_dither.at[i])

    @pl.when(core == 0)
    def _():
        start_stage(1, end_stage(0))
        start_stage(2, end_stage(1))
        value = end_stage(2)
        peak_send[4] = value
        to_core_1().start()
        peak_all[...] = value

    @pl.when(core == 1)
    def _():
        to_core_1().wait_recv()

    top = peak_all[...]
    top = jnp.max(jnp.max(top, axis=1, keepdims=True), axis=0, keepdims=True)
    peak = jnp.broadcast_to(top, (8, LANES))
    peak_ref[0] = LEVELS / peak
    peak_ref[1] = peak / (LEVELS * 16 * BLOCK)

    def codes(views, b, offsets):
        values = butterfly(parts_of(views, b))
        offsets = jnp.concatenate(offsets, axis=0)
        scale = peak_ref[0, 0:1, :]
        result = []
        for i in range(8):
            shift = offsets + ramp[:, lanes(i)]
            shift = shift - jnp.floor(shift)
            value = values[i // 2][:, (i % 2) * LANES:(i % 2 + 1) * LANES]
            result.append(jnp.floor(value * scale + shift))
        return result

    def own_codes(h, here, j, b, r0, n):
        targets = [target_of(h, here, j + jj) for jj in range(2)]
        rows = pl.ds(r0, n)
        return codes([held.at[c, rows, pl.ds(b * BLOCK, BLOCK)] for c in targets], b, [own_dither[c, rows, :] for c in targets])

    def near_codes(buffer, first, h, e, here, j, b, r0, n):
        targets = [target_of(h, here, j + jj) for jj in range(2)]
        views = [buffer.at[e, jj, pl.ds(first, n), :] for jj in range(2)]
        return codes(views, b, [near_dither[2 * h + e, c, pl.ds(r0, n), :] for c in targets])

    first_copies = {}

    def first(p):
        h, b, r0, n, q = PIECES[p]
        here = spots(h)[0]
        rows = pl.ds(q, n)
        for e in range(2):
            target = (here + 2 * e + 3) % SIDE
            for copy in raw_copies(p, e):
                copy.wait_recv()
            mine = own_codes(h, target, 2 * e, b, r0, n)
            other = near_codes(raw, q, h, e, target, 2 * e, b, r0, n)
            for i in range(8):
                total = (mine[i] + other[i]).astype(jnp.bfloat16)
                first_send[e, pl.ds(2 * e, 2), rows, lanes(i)] = total.reshape(2, n, LANES)
            if p not in LEAVES:
                mine = own_codes(h, target, 2 * (1 - e), b, r0, n)
                for i in range(8):
                    first_send[e, pl.ds(2 * (1 - e), 2), rows, lanes(i)] = mine[i].astype(jnp.bfloat16).reshape(2, n, LANES)
            sent = pl.ds(2 * e, 2) if p in LEAVES else slice(None)
            copy = pltpu.make_async_remote_copy(
                first_send.at[e, sent, rows, :], first_recv.at[e, sent, rows, :],
                first_ss.at[2 * p + e], first_rs.at[2 * p + e],
                device_id=neighbour(turns[h], 2 * e - 1), device_id_type=MESH)
            copy.start()
            first_copies[2 * p + e] = copy

    mid_copies, last_copies = {}, {}

    def combine(p):
        h, b, r0, n, q = PIECES[p]
        here, there = spots(h)
        rows = pl.ds(q, n)
        for e in range(2):
            first_copies[2 * p + e].wait_recv()

        def fill(half):
            pair = pl.ds(2 * half, 2)
            mine = own_codes(h, here, 2 * half, b, r0, n)
            if p in LEAVES:
                mine_too = near_codes(leaf, LEAVES[p], h, 1 - half, here, 2 * half, b, r0, n)
            for i in range(8):
                total = mine[i]
                if p in LEAVES:
                    total += mine_too[i] + first_recv[half, pair, rows, lanes(i)].astype(jnp.float32).reshape(2 * n, LANES)
                else:
                    for e in range(2):
                        total += first_recv[e, pair, rows, lanes(i)].astype(jnp.float32).reshape(2 * n, LANES)
                partial[pair, rows, lanes(i)] = total.astype(jnp.int32).astype(jnp.int16).reshape(2, n, LANES)

        def send():
            for e in range(2):
                copy = pltpu.make_async_remote_copy(
                    partial.at[(there + 2) % SIDE, rows, pl.ds(512 * e, 512)], second_raw.at[e, rows, :],
                    mid_ss.at[2 * p + e], mid_rs.at[2 * p + e],
                    device_id=neighbour(1 - turns[h], 2 * e - 1), device_id_type=MESH)
                copy.start()
                mid_copies[2 * p + e] = copy

        if p in LEAVES:
            for e in range(2):
                for copy in leaf_copies(p, e):
                    copy.wait_recv()
            fill(0)
            fill(1)
            send()
        else:
            opposite = (there + 2) % SIDE // 2
            fill(opposite)
            send()
            fill(1 - opposite)

    def forward(p):
        h, b, r0, n, q = PIECES[p]
        there = spots(h)[1]
        rows = pl.ds(q, n)
        for e in range(2):
            mid_copies[2 * p + e].wait_recv()
            j = (there + 2 * e + 3) % SIDE
            plain, summed = pl.ds(512 * (1 - e), 512), pl.ds(512 * e, 512)
            second_send[e, rows, plain] = partial[j, rows, plain]
            total = partial[j, rows, summed].astype(jnp.int32) + second_raw[e, rows, :].astype(jnp.int32)
            second_send[e, rows, summed] = total.astype(jnp.int16)
            copy = pltpu.make_async_remote_copy(
                second_send.at[e, rows, :], second_recv.at[e, rows, :],
                last_ss.at[2 * p + e], last_rs.at[2 * p + e],
                device_id=neighbour(1 - turns[h], 2 * e - 1), device_id_type=MESH)
            copy.start()
            last_copies[2 * p + e] = copy

    def decode(p):
        h, b, r0, n, q = PIECES[p]
        there = spots(h)[1]
        rows = pl.ds(q, n)
        for e in range(2):
            last_copies[2 * p + e].wait_recv()
        parts = []
        for k in range(SIDE):
            cols = pl.ds(k * SUB, SUB)
            total = partial[there, rows, cols].astype(jnp.int32)
            for e in range(2):
                total += second_recv[e, rows, cols].astype(jnp.int32)
            total = total.astype(jnp.float32)
            high = total.astype(jnp.bfloat16)
            low = (total - high.astype(jnp.float32)).astype(jnp.bfloat16)
            parts.append(jnp.dot(high, table[...], preferred_element_type=jnp.float32)
                         + jnp.dot(low, table[...], preferred_element_type=jnp.float32))
        values = butterfly(parts)
        factor = peak_ref[1, 0:1, :]
        for i in range(8):
            col = b * BLOCK + i * LANES
            flips = (1 - 2 * sign_ref[:, col:col + LANES]).astype(jnp.float32)
            value = values[i // 2][:, (i % 2) * LANES:(i % 2 + 1) * LANES]
            out_ref[r0:r0 + n, col:col + LANES] = (value * factor * flips).astype(jnp.bfloat16)

    tasks = (first, combine, forward, decode)
    for kind, step in ORDER:
        for p in (2 * step, 2 * step + 1):
            if p < len(PIECES):
                tasks[kind](p)
    for copies in (first_copies, mid_copies, last_copies):
        for copy in copies.values():
            copy.wait_send()
    for e in range(2):
        for copy in sum([raw_copies(p, e) for p in range(len(PIECES))], []) + sum([leaf_copies(p, e) for p in LEAVES], []):
            copy.wait_send()
    for copy in near_copies:
        copy.wait_send()

    @pl.when(core == 0)
    def _():
        for s in range(3):
            for copy in stage_copies(s):
                copy.wait_send()
        to_core_1().wait_send()

    @pl.when(core == 1)
    def _():
        from_core_1().wait_send()


def local(gradients, dither, sign_bits):
    row_count, col_count = gradients.shape[1:]
    grad = gradients.reshape(16, row_count // 16, col_count)
    vmem, dma = pltpu.VMEM, pltpu.SemaphoreType.DMA
    pieces = 2 * len(PIECES)
    return pl.pallas_call(
        kernel,
        out_shape=jax.ShapeDtypeStruct((row_count // 16, col_count), jnp.bfloat16),
        in_specs=[pl.BlockSpec(memory_space=pl.ANY)] * 2,
        out_specs=pl.BlockSpec(memory_space=pltpu.VMEM),
        scratch_shapes=[
            vmem((1, row_count), jnp.int32),
            vmem((1, col_count), jnp.int32),
            vmem((16, 144, col_count), jnp.bfloat16),
            vmem((3, SIDE, SUB, SUB), jnp.bfloat16),
            vmem((SUB, SUB), jnp.bfloat16),
            vmem((16, 144, LANES), jnp.float32),
            vmem((4, 24, LANES), jnp.int32),
            vmem((4, 16, 144, LANES), jnp.float32),
            vmem((24, LANES), jnp.int32),
            vmem((1, BLOCK), jnp.float32),
            vmem((5, 8, LANES), jnp.float32),
            vmem((10, 8, LANES), jnp.float32),
            vmem((8, LANES), jnp.float32),
            vmem((2, 8, LANES), jnp.float32),
            vmem((2, 2, ROWS, BLOCK), jnp.bfloat16),
            vmem((2, 2, LEAF_ROWS, BLOCK), jnp.bfloat16),
            vmem((2, SIDE, ROWS, BLOCK), jnp.bfloat16),
            vmem((2, SIDE, ROWS, BLOCK), jnp.bfloat16),
            vmem((SIDE, ROWS, BLOCK), jnp.int16),
            vmem((2, ROWS, 512), jnp.int16),
            vmem((2, ROWS, BLOCK), jnp.int16),
            vmem((2, ROWS, BLOCK), jnp.int16),
            dma((2,)), dma((16,)), dma((4,)), dma((4,)), dma((11,)), dma((11,)), dma((2 * pieces,)), dma((2 * pieces,)),
            dma((4 * len(LEAVES),)), dma((4 * len(LEAVES),)), dma((pieces,)), dma((pieces,)), dma((pieces,)), dma((pieces,)), dma((pieces,)), dma((pieces,)),
        ],
        compiler_params=pltpu.CompilerParams(collective_id=0, has_side_effects=True, vmem_limit_bytes=50 * 2**20),
    )(grad, jnp.concatenate([dither, sign_bits.reshape(1, col_count)], axis=1))


def solution(mesh):
    return jax.shard_map(
        local,
        mesh=mesh,
        in_specs=(P("dp", None, "tensor"), P("dp", None), P("tensor")),
        out_specs=P("dp", "tensor"),
        check_vma=False,
    )
```
